256 devices in a mesh: seq: 32 (over x, z), head: 8 (over y, core).
Axes of the slice: x: 4, y: 4, z: 8, core: 2. Of those that a mesh axis runs over, the one named last changes fastest.
Arguments:
- queries: bfloat16 [8192, 6144], P('seq', 'head'), may hold values from -32 to 32
- keys: bfloat16 [32768, 6144], P('seq', 'head'), may hold values from -32 to 32
- values: bfloat16 [32768, 6144], P('seq', 'head'), may hold values from -6 to 6
- query_cluster: int32 [8192], P('seq'), may hold values from 0 to 127, as said below
- key_cluster: int32 [32768], P('seq'), may hold values from 0 to 127, as said below
- cluster_owner: int32 [128], replicated, may hold values from 0 to 31, as said below
- pair_list: int32 [48, 128, 2], P('head'), may hold values from 0 to 127, as said below
- out_weight: bfloat16 [6144, 6144], P('head', 'seq'), may hold values from -0.15625 to 0.15625
Outputs:
- mixed: bfloat16 [8192, 6144], P('seq', 'head')
The draws below stay inside these ranges and needn't reach their ends.
Inputs may be any that keep to these rules, and one draw needn't show every extreme that they name: cluster_owner[query_cluster[i]] takes each seq index at most 16 times within each aligned block of 256 tokens; one owner takes exactly 16 in every block. cluster_owner[key_cluster[j]] takes each seq index at most 64 times within each aligned block of 1024 tokens; one owner takes exactly 64 in every block. `cluster_owner`: each seq index owns exactly 4 clusters. pair_list[h, a] names 2 distinct clusters, all owned by the owner of cluster a.
All inputs are finite; a program needn't handle non-finite values.
Results may differ from the reference program's by a relative error of at most 0.0057.
Values may be sent and summed in bfloat16 or wider, within the bound.
A program may use at most 128 MiB of HBM per device.

```python
import math
import jax
import jax.numpy as jnp
from jax import lax

HEADS = 48
HD = 128
D = 6144
Q_DEV = 256
K_DEV = 1024
CL_DEV = 4
PAIRS = 2
C = 128
QTOK = 8192
KTOK = 32768
N_SEQ = 32


def shared_layout(key):
    ordering = jax.random.permutation(jax.random.fold_in(key, 901), C)
    busiest = jax.random.randint(jax.random.fold_in(key, 902), (), 0, N_SEQ)
    return (ordering, busiest)


def block_owners(key, rows_dev, busiest):
    capacity = 2 * rows_dev // N_SEQ
    slot_owner = (jnp.arange(2 * rows_dev, dtype=jnp.int32) // capacity + busiest) % N_SEQ
    others = jax.random.permutation(key, 2 * rows_dev - capacity) + capacity
    chosen = jnp.concatenate([jnp.arange(capacity, dtype=jnp.int32), others[:rows_dev - capacity].astype(jnp.int32)])
    owners = slot_owner[chosen]
    mixing = jax.random.permutation(jax.random.fold_in(key, 1), rows_dev)
    return owners[mixing]


def token_clusters(key, rows_dev, ordering, busiest):
    owners = jax.vmap(lambda sub: block_owners(sub, rows_dev, busiest))(jax.random.split(key, N_SEQ)).reshape(-1)
    within = jax.random.randint(jax.random.fold_in(key, 11), (rows_dev * N_SEQ,), 0, CL_DEV)
    return ordering[owners * CL_DEV + within].astype(jnp.int32)


def draw_query_cluster(key, part):
    ordering, busiest = shared_layout(key)
    key = jax.random.fold_in(key, 3)
    return token_clusters(key, Q_DEV, ordering, busiest)


def draw_key_cluster(key, part):
    ordering, busiest = shared_layout(key)
    key = jax.random.fold_in(key, 4)
    return token_clusters(key, K_DEV, ordering, busiest)


def draw_cluster_owner(key, part):
    ordering, busiest = shared_layout(key)
    return (jnp.argsort(ordering) // CL_DEV).astype(jnp.int32)


def draw_pair_list(key, part):
    ordering, busiest = shared_layout(key)
    key = jax.random.fold_in(key, 6)
    owners = (jnp.argsort(ordering) // CL_DEV).astype(jnp.int32)
    picks = jax.vmap(lambda sub: jax.random.permutation(sub, CL_DEV)[:PAIRS])(jax.random.split(key, HEADS * C))
    picks = picks.reshape(HEADS, C, PAIRS).astype(jnp.int32)
    return ordering[owners[None, :, None] * CL_DEV + picks].astype(jnp.int32)


def draw_queries(key, part):
    key = jax.random.fold_in(key, 21)
    base = jax.random.normal(key, (QTOK, HEADS * HD), jnp.float32)
    return jnp.clip(base, -32.0, 32.0).astype(jnp.bfloat16)


def draw_keys(key, part):
    key = jax.random.fold_in(key, 22)
    base = jax.random.normal(key, (KTOK, HEADS * HD), jnp.float32)
    return jnp.clip(base, -32.0, 32.0).astype(jnp.bfloat16)


def spiked(array, key, source, target, blocks, factor):
    owner, partner = [(jnp.arange(array.shape[dim]) // (array.shape[dim] // blocks)).reshape([-1 if axis == dim else 1 for axis in range(array.ndim)]) for dim in (source, target)]
    chosen = jax.random.permutation(key, blocks)[partner]
    strong = (owner == chosen) | (owner == (partner + blocks // 2) % blocks)
    return jnp.where(strong, factor * array, array)


def block_scale(key, extent, shards, smallest, high):
    level = 1.0
    for dim, shards_of in shards:
        steps = jax.random.uniform(jax.random.fold_in(jax.random.fold_in(key, 6), dim), (shards_of,), jnp.float32, smallest / len(shards), high / len(shards))
        level = level * jnp.repeat(jnp.exp(steps), extent[dim] // shards_of).reshape((-1,) + (1,) * (len(extent) - 1 - dim))
    return level


def noise(stream_key, shape, scale, reach, pieces=(), kind=jnp.bfloat16):
    drawn = scale * jax.random.normal(stream_key, shape, jnp.float32)
    if pieces:
        drawn = drawn * block_scale(stream_key, shape, pieces, -0.22, 0.18)
    return jnp.clip(drawn, -reach, reach).astype(kind)


def bell_draw_with(own_key, extent, scale, bound, shards, heavy, held_as=jnp.bfloat16):
    values = scale * jax.random.normal(own_key, extent, jnp.float32)
    if shards:
        values = values * block_scale(own_key, extent, shards, -0.22, 0.18)
    return jnp.clip(spiked(values, jax.random.fold_in(own_key, 3), *heavy), -bound, bound).astype(held_as)


def setup_inputs(seed: int = 0) -> dict:
    arg_keys = jax.random.split(jax.random.key(seed), 9)
    return {
        "queries": draw_queries(jax.random.fold_in(arg_keys[8], 71), 0),
        "keys": draw_keys(jax.random.fold_in(arg_keys[8], 71), 0),
        "values": noise(arg_keys[2], (KTOK, HEADS * HD), 1.0, 6.0, ((0, 32), (1, 8))),
        "query_cluster": draw_query_cluster(jax.random.fold_in(arg_keys[8], 71), 0),
        "key_cluster": draw_key_cluster(jax.random.fold_in(arg_keys[8], 71), 0),
        "cluster_owner": draw_cluster_owner(jax.random.fold_in(arg_keys[8], 71), 0),
        "pair_list": draw_pair_list(jax.random.fold_in(arg_keys[8], 71), 0),
        "out_weight": bell_draw_with(arg_keys[7], (HEADS * HD, D), (HEADS * HD) ** -0.5, 0.15625, ((0, 8), (1, 32)), (0, 1, 32, 2.75)),
    }


def group_order(owner_ids, groups, width):
    order = jnp.argsort(owner_ids, stable=True).astype(jnp.int32)
    counts = lax.optimization_barrier(jnp.sum((owner_ids[:, None] == jnp.arange(groups, dtype=jnp.int32)[None, :]).astype(jnp.int32), axis=0))
    starts = (jnp.cumsum(counts) - counts).astype(jnp.int32)
    padded = jnp.concatenate([order, jnp.zeros((width,), jnp.int32)])
    return (padded, counts, starts)

def reference(queries, keys, values, query_cluster, key_cluster, cluster_owner, pair_list, out_weight):
    score_scale = 1.0 / math.sqrt(HD)
    listed = jnp.any(pair_list[:, :, :, None] == jnp.arange(C, dtype=jnp.int32)[None, None, None, :], axis=2)
    same_owner = cluster_owner[:, None] == cluster_owner[None, :]
    allowed = jnp.logical_and(listed, same_owner[None, :, :])
    query_width = 2 * Q_DEV
    key_width = 2 * K_DEV
    query_order, query_counts, query_starts = group_order(cluster_owner[query_cluster], N_SEQ, query_width)
    key_order, key_counts, key_starts = group_order(cluster_owner[key_cluster], N_SEQ, key_width)
    feature_width = HEADS * HD

    def one_owner(owner):
        query_index = lax.dynamic_slice_in_dim(query_order, query_starts[owner], query_width, 0).astype(jnp.int32)
        key_index = lax.dynamic_slice_in_dim(key_order, key_starts[owner], key_width, 0).astype(jnp.int32)
        query_valid = jnp.arange(query_width, dtype=jnp.int32) < query_counts[owner]
        key_valid = jnp.arange(key_width, dtype=jnp.int32) < key_counts[owner]
        query_rows = jnp.transpose(queries[query_index].reshape(query_width, HEADS, HD), (1, 0, 2))
        key_rows = jnp.transpose(keys[key_index].reshape(key_width, HEADS, HD), (1, 0, 2))
        value_rows = jnp.transpose(values[key_index].reshape(key_width, HEADS, HD), (1, 0, 2))
        query_labels = query_cluster[query_index]
        key_labels = key_cluster[key_index]

        def one_head(operands):
            query_part, key_part, value_part, pair_table = operands
            visible = jnp.logical_and(pair_table[query_labels][:, key_labels], key_valid[None, :])
            scores = jnp.dot(query_part, key_part.T, preferred_element_type=jnp.float32) * score_scale
            largest = jnp.maximum(lax.optimization_barrier(jnp.max(jnp.where(visible, scores, -jnp.inf), axis=1)), 0.0)
            weights = jnp.where(visible, jnp.exp(scores - largest[:, None]), 0.0)
            total = jnp.exp(-largest) + lax.optimization_barrier(jnp.sum(weights, axis=1))
            probs = (weights / total[:, None]).astype(jnp.bfloat16)
            return jnp.dot(probs, value_part, preferred_element_type=jnp.float32).astype(jnp.bfloat16)
        outputs = lax.map(one_head, (query_rows, key_rows, value_rows, allowed))
        rows_out = jnp.transpose(outputs, (1, 0, 2)).reshape(query_width, feature_width)
        target = jnp.where(query_valid, query_index, QTOK).astype(jnp.int32)
        return (rows_out, target)
    owner_rows, owner_targets = lax.map(one_owner, jnp.arange(N_SEQ, dtype=jnp.int32))
    attended = jnp.zeros((QTOK, feature_width), jnp.bfloat16).at[owner_targets.reshape(-1)].set(owner_rows.reshape(-1, feature_width), mode='drop')
    return jnp.dot(attended, out_weight, preferred_element_type=jnp.float32).astype(jnp.bfloat16)
```

```python
import functools
import math

import jax
import jax.numpy as jnp
from jax import lax
from jax.experimental import pallas as pl
from jax.experimental.pallas import tpu as pltpu
from jax.sharding import PartitionSpec as P

MESH = pl.DeviceIdType.MESH
HEAD_SIZE = 128
MASKED = -float(2**20)
CHUNK = 256

Q, LAB, K, V, O = range(5)


def iota(shape, dim):
    return lax.broadcasted_iota(jnp.int32, shape, dim)


def hot(mask):
    return jnp.where(mask, 1.0, 0.0).astype(jnp.bfloat16)


def dot_nt(a, b):
    return lax.dot_general(a, b, (((1,), (1,)), ((), ())), preferred_element_type=jnp.float32)


def dot_tn(a, b):
    return lax.dot_general(a, b, (((0,), (0,)), ((), ())), preferred_element_type=jnp.float32)


def relative_slots(label_ref, owner_rows, me, n, capacity, slot_ref):
    clusters = owner_rows.shape[1]
    upper = hot(iota((128, 128), 0) <= iota((128, 128), 1))
    seen = jnp.zeros((n, 1), jnp.float32)
    for start in range(0, label_ref.shape[1], 128):
        labels = label_ref[0:1, start : start + 128]
        cluster_hot = hot(iota((clusters, 128), 0) == labels)
        owner = jnp.dot(owner_rows, cluster_hot, preferred_element_type=jnp.float32)[0:1]
        relative = owner.astype(jnp.int32) - me
        relative = jnp.where(relative < 0, relative + n, relative)
        match = iota((n, 128), 0) == relative
        owner_hot = jnp.where(match, 1.0, 0.0)
        counts = jnp.dot(
            owner_hot.astype(jnp.bfloat16), upper, preferred_element_type=jnp.float32
        )
        rank = jnp.sum(jnp.where(match, counts + seen, 0.0), axis=0, keepdims=True) - 1.0
        slot_ref[0:1, start : start + 128] = relative * capacity + rank.astype(jnp.int32)
        seen = seen + jnp.sum(owner_hot, axis=1, keepdims=True)


def exchange_kernel(
    n, q_ref, k_ref, v_ref, qc_ref, kc_ref, owner_ref, bias_ref, out_ref,
    sq, rq, slab, rlab, sk, rk, sv, rv, so, ro, q_slot, k_slot, key_hot, probs, inverse,
    send_sem, recv_sem,
):
    me = lax.axis_index("seq")
    q_rows, k_rows = q_ref.shape[0], k_ref.shape[0]
    q_cap, k_cap = 2 * q_rows // n, 2 * k_rows // n
    heads, clusters = bias_ref.shape[0], bias_ref.shape[1]
    per_chunk = CHUNK // k_cap
    slots_q, slots_k = n * q_cap, n * k_cap

    def peer(i):
        return lax.rem(me + i, n)

    def copy(kind, i):
        source, target, rows = {
            Q: (sq, rq, q_cap), K: (sk, rk, k_cap), V: (sv, rv, k_cap),
            O: (so, ro, q_cap), LAB: (slab, rlab, 0),
        }[kind]
        if rows:
            window = pl.ds(pl.multiple_of(i * rows, rows), rows)
        else:
            window = i
        return pltpu.make_async_remote_copy(
            src_ref=source.at[window],
            dst_ref=target.at[window],
            send_sem=send_sem.at[kind, i],
            recv_sem=recv_sem.at[kind, i],
            device_id={"seq": peer(n - i) if kind == O else peer(i)},
            device_id_type=MESH,
        )

    barrier = pltpu.get_barrier_semaphore()

    @pl.loop(1, n)
    def _(i):
        pl.semaphore_signal(barrier, inc=1, device_id={"seq": peer(i)}, device_id_type=MESH)

    owner_rows = jnp.broadcast_to(
        owner_ref[...].astype(jnp.float32), (8, clusters)
    ).astype(jnp.bfloat16)
    relative_slots(qc_ref, owner_rows, me, n, q_cap, q_slot)
    relative_slots(kc_ref, owner_rows, me, n, k_cap, k_slot)

    pack_q = hot(iota((slots_q, q_rows), 0) == q_slot[...])
    sq[...] = jnp.dot(pack_q, q_ref[...], preferred_element_type=jnp.float32).astype(sq.dtype)
    q_labels = jnp.broadcast_to(
        (qc_ref[...] + 1).astype(jnp.float32), (8, q_rows)
    ).astype(jnp.bfloat16)
    packed = dot_nt(q_labels, pack_q)
    per_row = 128 // q_cap
    for i in range(n):
        group = i // per_row * 128
        slab[i, 1:2, :] = packed[0:1, group : group + 128]
    k_labels = jnp.broadcast_to(
        (kc_ref[...] + 1).astype(jnp.float32), (8, k_rows)
    ).astype(jnp.bfloat16)

    pl.semaphore_wait(barrier, n - 1)

    @pl.loop(0, slots_k // CHUNK)
    def _(j):
        base = pl.multiple_of(j * CHUNK, CHUNK)
        pack = hot(iota((CHUNK, k_rows), 0) + base == k_slot[...])
        sk[pl.ds(base, CHUNK), :] = jnp.dot(
            pack, k_ref[...], preferred_element_type=jnp.float32
        ).astype(sk.dtype)
        labels = dot_nt(k_labels, pack)
        for t in range(per_chunk):
            first = t * k_cap // 128 * 128
            slab[j * per_chunk + t, 0:1, :] = labels[0:1, first : first + 128]
        for t in range(per_chunk):
            i = j * per_chunk + t

            @pl.when(i > 0)
            def _():
                copy(LAB, i).start()
                copy(Q, i).start()
                copy(K, i).start()

    @pl.loop(0, slots_k // CHUNK)
    def _(j):
        base = pl.multiple_of(j * CHUNK, CHUNK)
        pack = hot(iota((CHUNK, k_rows), 0) + base == k_slot[...])
        sv[pl.ds(base, CHUNK), :] = jnp.dot(
            pack, v_ref[...], preferred_element_type=jnp.float32
        ).astype(sv.dtype)
        for t in range(per_chunk):
            i = j * per_chunk + t

            @pl.when(i > 0)
            def _():
                copy(V, i).start()

    rq[0:q_cap, :] = sq[0:q_cap, :]
    rk[0:k_cap, :] = sk[0:k_cap, :]
    rv[0:k_cap, :] = sv[0:k_cap, :]
    rlab[0] = slab[0]

    @pl.loop(1, n)
    def _(i):
        copy(LAB, i).wait_recv()
        copy(Q, i).wait_recv()
        copy(K, i).wait_recv()

    lane = iota((1, 128), 1)
    q_row = []
    for first in range(0, n, per_row):
        row = jnp.zeros((1, 128), jnp.float32)
        for i in range(first, first + per_row):
            row = jnp.where(lane // q_cap == i % per_row, rlab[i, 1:2, :], row)
        q_row.append(row)
    query_hot = [
        hot(iota((clusters, 128), 0) == row.astype(jnp.int32) - 1) for row in q_row
    ]
    query_hot = jnp.concatenate(query_hot, axis=1)
    per_lanes = 128 // k_cap
    for first in range(0, n, per_lanes):
        row = rlab[first, 0:1, :]
        for i in range(first + 1, first + per_lanes):
            row = jnp.where(lane // k_cap == i % per_lanes, rlab[i, 0:1, :], row)
        row = row.astype(jnp.int32) - 1
        key_hot[:, first * k_cap : first * k_cap + 128] = hot(
            (iota((clusters, 128), 0) == row) | (row < 0)
        )

    exponent = 1.0 / math.sqrt(HEAD_SIZE) / math.log(2.0)
    half = slots_q // 2

    def columns(h):
        return pl.ds(pl.multiple_of(h * HEAD_SIZE, HEAD_SIZE), HEAD_SIZE)

    @pl.loop(0, heads)
    def _(h):
        selected = dot_tn(query_hot, bias_ref[h]).astype(jnp.bfloat16)
        for part in range(2):
            rows = slice(part * half, (part + 1) * half)
            scores = dot_nt(rq[rows, columns(h)], rk[:, columns(h)])
            scores = scores + jnp.dot(
                selected[rows], key_hot[...], preferred_element_type=jnp.float32
            )
            largest = jnp.maximum(jnp.max(scores, axis=1, keepdims=True), 0.0)
            weights = jnp.exp2((scores - largest) * exponent)
            total = jnp.exp2(-largest * exponent) + jnp.sum(weights, axis=1, keepdims=True)
            probs[h, rows, :] = weights.astype(jnp.bfloat16)
            inverse[h, rows, :] = 1.0 / total

    @pl.loop(1, n)
    def _(i):
        copy(V, i).wait_recv()

    @pl.loop(0, heads)
    def _(h):
        so[:, columns(h)] = (
            jnp.dot(probs[h], rv[:, columns(h)], preferred_element_type=jnp.float32)
            * inverse[h]
        ).astype(so.dtype)

    @pl.loop(1, n)
    def _(i):
        copy(O, i).start()

    ro[0:q_cap, :] = so[0:q_cap, :]

    @pl.loop(1, n)
    def _(i):
        copy(O, i).wait_recv()

    unpack = hot(iota((slots_q, q_rows), 0) == q_slot[...])
    out_ref[...] = dot_tn(unpack, ro[...]).astype(out_ref.dtype)

    @pl.loop(1, n)
    def _(i):
        for kind in (LAB, Q, K, V, O):
            copy(kind, i).wait_send()


def attend(queries, keys, values, query_cluster, key_cluster, cluster_owner, bias):
    n = lax.axis_size("seq")
    q_rows, width = queries.shape
    k_rows = keys.shape[0]
    slots_q, slots_k = 2 * q_rows, 2 * k_rows
    heads, clusters = bias.shape[0], bias.shape[1]
    vmem = pl.BlockSpec(memory_space=pltpu.VMEM)

    def rows(count):
        return pltpu.VMEM((count, width), jnp.bfloat16)

    return pl.pallas_call(
        functools.partial(exchange_kernel, n),
        out_shape=jax.ShapeDtypeStruct((q_rows, width), jnp.bfloat16),
        in_specs=[vmem] * 7,
        out_specs=vmem,
        scratch_shapes=[
            rows(slots_q), rows(slots_q),
            pltpu.VMEM((n, 8, 128), jnp.float32), pltpu.VMEM((n, 8, 128), jnp.float32),
            rows(slots_k), rows(slots_k), rows(slots_k), rows(slots_k),
            rows(slots_q), rows(slots_q),
            pltpu.VMEM((1, q_rows), jnp.int32), pltpu.VMEM((1, k_rows), jnp.int32),
            pltpu.VMEM((clusters, slots_k), jnp.bfloat16),
            pltpu.VMEM((heads, slots_q, slots_k), jnp.bfloat16),
            pltpu.VMEM((heads, slots_q, 1), jnp.float32),
            pltpu.SemaphoreType.DMA((5, n)), pltpu.SemaphoreType.DMA((5, n)),
        ],
        compiler_params=pltpu.CompilerParams(
            collective_id=0, has_side_effects=True, vmem_limit_bytes=48 * 2**20
        ),
        cost_estimate=pl.CostEstimate(
            flops=2 * 10**11, bytes_accessed=16 * 2**20, transcendentals=0
        ),
    )(queries, keys, values, query_cluster[None], key_cluster[None], cluster_owner[None], bias)


def per_device(
    queries, keys, values, query_cluster, key_cluster, cluster_owner, pair_list, out_weight
):
    clusters = cluster_owner.shape[0]
    listed = jnp.any(
        pair_list[:, :, :, None] == jnp.arange(clusters, dtype=jnp.int32)[None, None, None, :],
        axis=2,
    )
    bias = jnp.where(listed, 0.0, MASKED).astype(jnp.bfloat16)
    attended = attend(
        queries, keys, values, query_cluster, key_cluster, cluster_owner, bias
    )
    terms = jnp.dot(
        attended,
        lax.all_gather(out_weight, "seq", axis=1, tiled=True),
        preferred_element_type=jnp.float32,
    )
    return lax.psum_scatter(terms, "head", scatter_dimension=1, tiled=True).astype(jnp.bfloat16)


def solution(mesh):
    in_specs = (
        P("seq", "head"),
        P("seq", "head"),
        P("seq", "head"),
        P("seq"),
        P("seq"),
        P(),
        P("head", None, None),
        P("head", "seq"),
    )
    out_specs = P("seq", "head")
    return jax.shard_map(
        per_device, mesh=mesh, in_specs=in_specs, out_specs=out_specs, check_vma=False
    )
```

```python
import functools
import math

import jax
import jax.numpy as jnp
from jax import lax
from jax.experimental import pallas as pl
from jax.experimental.pallas import tpu as pltpu
from jax.sharding import PartitionSpec as P

MESH = pl.DeviceIdType.MESH
HEAD_SIZE = 128
MASKED = -float(2**20)
CHUNK = 256

Q, LAB, K, V, O = range(5)
X_SIZE = 4


def iota(shape, dim):
    return lax.broadcasted_iota(jnp.int32, shape, dim)


def hot(mask):
    return jnp.where(mask, 1.0, 0.0).astype(jnp.bfloat16)


def dot_nt(a, b):
    return lax.dot_general(a, b, (((1,), (1,)), ((), ())), preferred_element_type=jnp.float32)


def dot_tn(a, b):
    return lax.dot_general(a, b, (((0,), (0,)), ((), ())), preferred_element_type=jnp.float32)


def offset(i, n):
    z_size = n // X_SIZE
    a, k = i // z_size, lax.rem(i, z_size)
    dz = (k + 1) // 2 * (2 * lax.rem(k, 2) - 1)
    return lax.rem(a + k, X_SIZE), dz


def order_of(owner, me, n):
    z_size = n // X_SIZE
    dx = (owner // z_size - me // z_size) & (X_SIZE - 1)
    dz = (owner - me) & (z_size - 1)
    k = jnp.where(dz <= z_size // 2, jnp.maximum(2 * dz - 1, 0), 2 * (z_size - dz))
    return ((dx - k) & (X_SIZE - 1)) * z_size + k


def relative_slots(label_ref, owner_rows, me, n, capacity, slot_ref):
    clusters = owner_rows.shape[1]
    upper = hot(iota((128, 128), 0) <= iota((128, 128), 1))
    seen = jnp.zeros((n, 1), jnp.float32)
    for start in range(0, label_ref.shape[1], 128):
        labels = label_ref[0:1, start : start + 128]
        cluster_hot = hot(iota((clusters, 128), 0) == labels)
        owner = jnp.dot(owner_rows, cluster_hot, preferred_element_type=jnp.float32)[0:1]
        relative = order_of(owner.astype(jnp.int32), me, n)
        match = iota((n, 128), 0) == relative
        owner_hot = jnp.where(match, 1.0, 0.0)
        counts = jnp.dot(
            owner_hot.astype(jnp.bfloat16), upper, preferred_element_type=jnp.float32
        )
        rank = jnp.sum(jnp.where(match, counts + seen, 0.0), axis=0, keepdims=True) - 1.0
        slot_ref[0:1, start : start + 128] = relative * capacity + rank.astype(jnp.int32)
        seen = seen + jnp.sum(owner_hot, axis=1, keepdims=True)


def exchange_kernel(
    n, n_head, q_ref, k_ref, v_ref, w_ref, qc_ref, kc_ref, owner_ref, bias_ref, out_ref,
    sq, rq, slab, rlab, sk, rk, sv, rv, so, ro, q_slot, k_slot, key_hot, probs,
    pieces, weight, mixed_in,
    send_sem, recv_sem, piece_send, piece_recv, w_send, w_recv, a_send, a_recv,
):
    me = lax.axis_index("seq")
    head = lax.axis_index("head")
    parts = n // n_head
    depth = w_ref.shape[0] // parts
    z_size = n // X_SIZE
    x, z = me // z_size, lax.rem(me, z_size)
    q_rows, k_rows = q_ref.shape[0], k_ref.shape[0]
    q_cap, k_cap = 2 * q_rows // n, 2 * k_rows // n
    heads, clusters = bias_ref.shape[0], bias_ref.shape[1]
    per_chunk = CHUNK // k_cap
    slots_q, slots_k = n * q_cap, n * k_cap

    def at(dx, dz):
        return lax.rem(x + dx + X_SIZE, X_SIZE) * z_size + lax.rem(z + dz + z_size, z_size)

    def peer(i, sign=1):
        dx, dz = offset(i, n)
        return at(sign * dx, sign * dz)

    def copy(kind, i):
        source, target, rows = {
            Q: (sq, rq, q_cap), K: (sk, rk, k_cap), V: (sv, rv, k_cap),
            O: (so, ro, q_cap), LAB: (slab, rlab, 0),
        }[kind]
        if rows:
            window = pl.ds(pl.multiple_of(i * rows, rows), rows)
        else:
            window = i
        return pltpu.make_async_remote_copy(
            src_ref=source.at[window],
            dst_ref=target.at[window],
            send_sem=send_sem.at[kind, i],
            recv_sem=recv_sem.at[kind, i],
            device_id={"seq": peer(i, -1) if kind == O else peer(i)},
            device_id_type=MESH,
        )

    here = me // parts == head

    def piece_copy(j):
        return pltpu.make_async_remote_copy(
            src_ref=w_ref.at[pl.ds(j * depth, depth)],
            dst_ref=pieces.at[lax.rem(me, parts)],
            send_sem=piece_send.at[j],
            recv_sem=piece_recv.at[lax.rem(me, parts)],
            device_id={"seq": parts * head + j, "head": me // parts},
            device_id_type=MESH,
        )

    def piece_stays(j):
        return here & (lax.rem(me, parts) == j)

    def piece_local(j):
        return pltpu.make_async_copy(
            w_ref.at[pl.ds(j * depth, depth)], pieces.at[j], piece_recv.at[j]
        )

    def weight_copy(block, target, index):
        window = pl.ds(pl.multiple_of(block * depth, depth), depth)
        return pltpu.make_async_remote_copy(
            src_ref=weight.at[window],
            dst_ref=weight.at[window],
            send_sem=w_send.at[index],
            recv_sem=w_recv.at[block],
            device_id={"seq": target},
            device_id_type=MESH,
        )

    far = z_size // 2
    z_first = [(0, 1), (0, -1), (0, far)]
    z_second = [(-1, 1), (1, -1), (far, 1), (far, -1)]

    def z_first_copy(i):
        return weight_copy(me, at(0, z_first[i][1]), i)

    def z_second_copy(i):
        return weight_copy(at(0, z_second[i][0]), at(0, z_second[i][1]), 3 + i)

    def x_first_copy(dz, i):
        return weight_copy(at(0, dz), at(1 - 2 * i, 0), 7 + 2 * (dz % z_size) + i)

    def x_second_copy(dz):
        step = 1 - 2 * (dz % 2)
        return weight_copy(at(-step, dz), at(step, 0), 7 + 2 * z_size + dz % z_size)

    def wait_block(block):
        weight_copy(block, me, 0).wait_recv()

    z_near = [0, 1, -1, far]
    z_later = [2, -2, 3, -3]

    mate = head + 1 - 2 * lax.rem(head, 2)

    def along(t):
        return lax.rem(head + 2 * t, n_head)

    def block_copy(block, target, index):
        return pltpu.make_async_remote_copy(
            src_ref=mixed_in.at[block],
            dst_ref=mixed_in.at[block],
            send_sem=a_send.at[index],
            recv_sem=a_recv.at[block],
            device_id={"head": target},
            device_id_type=MESH,
        )

    barrier = pltpu.get_barrier_semaphore()
    ys = n_head // 2
    for t in range(1, ys):
        pl.semaphore_signal(barrier, inc=1, device_id={"head": along(t)}, device_id_type=MESH)
    pl.semaphore_signal(barrier, inc=1, device_id={"head": mate}, device_id_type=MESH)
    for j in range(parts):

        @pl.when(jnp.logical_not(piece_stays(j)))
        def _():
            pl.semaphore_signal(
                barrier, inc=1, device_id={"seq": parts * head + j, "head": me // parts},
                device_id_type=MESH,
            )

    @pl.loop(1, n)
    def _(i):
        pl.semaphore_signal(barrier, inc=1, device_id={"seq": peer(i)}, device_id_type=MESH)

    owner_rows = jnp.broadcast_to(
        owner_ref[...].astype(jnp.float32), (8, clusters)
    ).astype(jnp.bfloat16)
    relative_slots(qc_ref, owner_rows, me, n, q_cap, q_slot)
    relative_slots(kc_ref, owner_rows, me, n, k_cap, k_slot)

    pack_q = hot(iota((slots_q, q_rows), 0) == q_slot[...])
    sq[...] = jnp.dot(pack_q, q_ref[...], preferred_element_type=jnp.float32).astype(sq.dtype)
    q_labels = jnp.broadcast_to(
        (qc_ref[...] + 1).astype(jnp.float32), (8, q_rows)
    ).astype(jnp.bfloat16)
    packed = dot_nt(q_labels, pack_q)
    per_row = 128 // q_cap
    for i in range(n):
        group = i // per_row * 128
        slab[i, 1:2, :] = packed[0:1, group : group + 128]
    k_labels = jnp.broadcast_to(
        (kc_ref[...] + 1).astype(jnp.float32), (8, k_rows)
    ).astype(jnp.bfloat16)

    @pl.when(here)
    def _():
        pl.semaphore_wait(barrier, n - 1 + ys + parts - 1)

    @pl.when(jnp.logical_not(here))
    def _():
        pl.semaphore_wait(barrier, n - 1 + ys + parts)

    for j in range(parts):

        @pl.when(piece_stays(j))
        def _():
            piece_local(j).start()

        @pl.when(jnp.logical_not(piece_stays(j)))
        def _():
            piece_copy(j).start()

    @pl.loop(0, slots_k // CHUNK)
    def _(j):
        base = pl.multiple_of(j * CHUNK, CHUNK)
        pack = hot(iota((CHUNK, k_rows), 0) + base == k_slot[...])
        sk[pl.ds(base, CHUNK), :] = jnp.dot(
            pack, k_ref[...], preferred_element_type=jnp.float32
        ).astype(sk.dtype)
        labels = dot_nt(k_labels, pack)
        for t in range(per_chunk):
            first = t * k_cap // 128 * 128
            slab[j * per_chunk + t, 0:1, :] = labels[0:1, first : first + 128]
        for t in range(per_chunk):
            i = j * per_chunk + t

            @pl.when(i > 0)
            def _():
                copy(LAB, i).start()
                copy(Q, i).start()
                copy(K, i).start()

    for j in range(parts):
        piece_local(j).wait()
    weight[pl.ds(pl.multiple_of(me * depth, depth), depth), :] = jnp.concatenate(
        [pieces[j] for j in range(parts)], axis=1
    )
    for i in range(3):
        z_first_copy(i).start()

    def send_values(first, last):
        @pl.loop(first, last)
        def _(j):
            base = pl.multiple_of(j * CHUNK, CHUNK)
            pack = hot(iota((CHUNK, k_rows), 0) + base == k_slot[...])
            sv[pl.ds(base, CHUNK), :] = jnp.dot(
                pack, v_ref[...], preferred_element_type=jnp.float32
            ).astype(sv.dtype)
            for t in range(per_chunk):
                i = j * per_chunk + t

                @pl.when(i > 0)
                def _():
                    copy(V, i).start()

    chunks = slots_k // CHUNK
    send_values(0, chunks // 2)
    for dz in (1, -1, far):
        wait_block(at(0, dz))
    for i in range(4):
        z_second_copy(i).start()
    for dz in z_near:
        for i in range(2):
            x_first_copy(dz, i).start()
    send_values(chunks // 2, chunks)
    for dz in z_later:
        wait_block(at(0, dz))
    for dz in z_later:
        for i in range(2):
            x_first_copy(dz, i).start()

    rq[0:q_cap, :] = sq[0:q_cap, :]
    rk[0:k_cap, :] = sk[0:k_cap, :]
    rv[0:k_cap, :] = sv[0:k_cap, :]
    rlab[0] = slab[0]

    @pl.loop(1, n)
    def _(i):
        copy(LAB, i).wait_recv()
        copy(Q, i).wait_recv()
        copy(K, i).wait_recv()

    lane = iota((1, 128), 1)
    q_row = []
    for first in range(0, n, per_row):
        row = jnp.zeros((1, 128), jnp.float32)
        for i in range(first, first + per_row):
            row = jnp.where(lane // q_cap == i % per_row, rlab[i, 1:2, :], row)
        q_row.append(row)
    query_hot = [
        hot(iota((clusters, 128), 0) == row.astype(jnp.int32) - 1) for row in q_row
    ]
    query_hot = jnp.concatenate(query_hot, axis=1)
    per_lanes = 128 // k_cap
    for first in range(0, n, per_lanes):
        row = rlab[first, 0:1, :]
        for i in range(first + 1, first + per_lanes):
            row = jnp.where(lane // k_cap == i % per_lanes, rlab[i, 0:1, :], row)
        row = row.astype(jnp.int32) - 1
        key_hot[:, first * k_cap : first * k_cap + 128] = hot(
            (iota((clusters, 128), 0) == row) | (row < 0)
        )

    exponent = 1.0 / math.sqrt(HEAD_SIZE) / math.log(2.0)
    half = slots_q // 2

    def columns(h):
        return pl.ds(pl.multiple_of(h * HEAD_SIZE, HEAD_SIZE), HEAD_SIZE)

    @pl.loop(0, heads)
    def _(h):
        selected = dot_tn(query_hot, bias_ref[h]).astype(jnp.bfloat16)
        for part in range(2):
            rows = slice(part * half, (part + 1) * half)
            scores = dot_nt(rq[rows, columns(h)], rk[:, columns(h)])
            scores = scores + jnp.dot(
                selected[rows], key_hot[...], preferred_element_type=jnp.float32
            )
            largest = jnp.maximum(jnp.max(scores, axis=1, keepdims=True), 0.0)
            weights = jnp.exp2((scores - largest) * exponent)
            total = jnp.exp2(-largest * exponent) + jnp.sum(weights, axis=1, keepdims=True)
            probs[h, rows, :] = (weights * (1.0 / total)).astype(jnp.bfloat16)

    for dz in z_near + z_later:
        wait_block(at(1, dz))
        wait_block(at(-1, dz))
        x_second_copy(dz).start()

    @pl.loop(1, n)
    def _(i):
        copy(V, i).wait_recv()

    @pl.loop(0, heads)
    def _(h):
        so[:, columns(h)] = jnp.dot(
            probs[h], rv[:, columns(h)], preferred_element_type=jnp.float32
        ).astype(so.dtype)

    @pl.loop(1, n)
    def _(i):
        copy(O, i).start()

    ro[0:q_cap, :] = so[0:q_cap, :]

    @pl.loop(1, n)
    def _(i):
        copy(O, i).wait_recv()

    unpack = hot(iota((slots_q, q_rows), 0) == q_slot[...])
    mixed_in[head] = dot_tn(unpack, ro[...]).astype(mixed_in.dtype)
    for t in range(1, ys):
        block_copy(head, along(t), t - 1).start()
    block_copy(head, mate, ys - 1).start()

    for dz in z_near + z_later:
        wait_block(at(2, dz))

    def product(block):
        width = mixed_in.shape[2]
        return jnp.dot(
            mixed_in[block], weight[pl.ds(pl.multiple_of(block * width, width), width), :],
            preferred_element_type=jnp.float32,
        )

    total = product(head)
    for t in range(1, ys):
        block_copy(along(t), mate, 0).wait_recv()
        block_copy(along(t), mate, ys - 1 + t).start()
        total = total + product(along(t))
    for t in range(ys):
        block = lax.rem(mate + 2 * t, n_head)
        block_copy(block, mate, 0).wait_recv()
        total = total + product(block)
    out_ref[...] = total.astype(out_ref.dtype)

    @pl.loop(1, n)
    def _(i):
        for kind in (LAB, Q, K, V, O):
            copy(kind, i).wait_send()

    for j in range(parts):

        @pl.when(jnp.logical_not(piece_stays(j)))
        def _():
            piece_copy(j).wait_send()

    for i in range(3):
        z_first_copy(i).wait_send()
    for i in range(4):
        z_second_copy(i).wait_send()
    for dz in range(z_size):
        for i in range(2):
            x_first_copy(dz, i).wait_send()
        x_second_copy(dz).wait_send()
    for t in range(1, ys):
        block_copy(head, along(t), t - 1).wait_send()
        block_copy(along(t), mate, ys - 1 + t).wait_send()
    block_copy(head, mate, ys - 1).wait_send()


def mix(queries, keys, values, out_weight, query_cluster, key_cluster, cluster_owner, bias):
    n, n_head = lax.axis_size("seq"), lax.axis_size("head")
    parts = n // n_head
    depth, narrow = out_weight.shape[0] // parts, out_weight.shape[1]
    q_rows, width = queries.shape
    k_rows = keys.shape[0]
    slots_q, slots_k = 2 * q_rows, 2 * k_rows
    heads, clusters = bias.shape[0], bias.shape[1]
    vmem = pl.BlockSpec(memory_space=pltpu.VMEM)

    def rows(count):
        return pltpu.VMEM((count, width), jnp.bfloat16)

    return pl.pallas_call(
        functools.partial(exchange_kernel, n, n_head),
        out_shape=jax.ShapeDtypeStruct((q_rows, narrow * parts), jnp.bfloat16),
        in_specs=[vmem] * 8,
        out_specs=vmem,
        scratch_shapes=[
            rows(slots_q), rows(slots_q),
            pltpu.VMEM((n, 8, 128), jnp.float32), pltpu.VMEM((n, 8, 128), jnp.float32),
            rows(slots_k), rows(slots_k), rows(slots_k), rows(slots_k),
            rows(slots_q), rows(slots_q),
            pltpu.VMEM((1, q_rows), jnp.int32), pltpu.VMEM((1, k_rows), jnp.int32),
            pltpu.VMEM((clusters, slots_k), jnp.bfloat16),
            pltpu.VMEM((heads, slots_q, slots_k), jnp.bfloat16),
            pltpu.VMEM((parts, depth, narrow), jnp.bfloat16),
            pltpu.VMEM((depth * n, narrow * parts), jnp.bfloat16),
            pltpu.VMEM((n_head, q_rows, width), jnp.bfloat16),
            pltpu.SemaphoreType.DMA((5, n)), pltpu.SemaphoreType.DMA((5, n)),
            pltpu.SemaphoreType.DMA((parts,)), pltpu.SemaphoreType.DMA((parts,)),
            pltpu.SemaphoreType.DMA((n + 7,)), pltpu.SemaphoreType.DMA((n,)),
            pltpu.SemaphoreType.DMA((n_head,)), pltpu.SemaphoreType.DMA((n_head,)),
        ],
        compiler_params=pltpu.CompilerParams(
            collective_id=0, has_side_effects=True, vmem_limit_bytes=60 * 2**20
        ),
        cost_estimate=pl.CostEstimate(
            flops=2 * 10**11, bytes_accessed=16 * 2**20, transcendentals=0
        ),
    )(
        queries, keys, values, out_weight, query_cluster[None], key_cluster[None],
        cluster_owner[None], bias,
    )


def per_device(
    queries, keys, values, query_cluster, key_cluster, cluster_owner, pair_list, out_weight
):
    clusters = cluster_owner.shape[0]
    listed = jnp.any(
        pair_list[:, :, :, None] == jnp.arange(clusters, dtype=jnp.int32)[None, None, None, :],
        axis=2,
    )
    bias = jnp.where(listed, 0.0, MASKED).astype(jnp.bfloat16)
    return mix(
        queries, keys, values, out_weight, query_cluster, key_cluster, cluster_owner, bias
    )


def solution(mesh):
    in_specs = (
        P("seq", "head"),
        P("seq", "head"),
        P("seq", "head"),
        P("seq"),
        P("seq"),
        P(),
        P("head", None, None),
        P("head", "seq"),
    )
    out_specs = P("seq", "head")
    return jax.shard_map(
        per_device, mesh=mesh, in_specs=in_specs, out_specs=out_specs, check_vma=False
    )
```

```python
import functools
import math

import jax
import jax.numpy as jnp
from jax import lax
from jax.experimental import pallas as pl
from jax.experimental.pallas import tpu as pltpu
from jax.sharding import PartitionSpec as P

MESH = pl.DeviceIdType.MESH
HEAD_SIZE = 128
MASKED = -float(2**20)
CHUNK = 256

Q, LAB, K, V, O = range(5)
X_SIZE = 4


def iota(shape, dim):
    return lax.broadcasted_iota(jnp.int32, shape, dim)


def hot(mask):
    return jnp.where(mask, 1.0, 0.0).astype(jnp.bfloat16)


def dot_nt(a, b):
    return lax.dot_general(a, b, (((1,), (1,)), ((), ())), preferred_element_type=jnp.float32)


def dot_tn(a, b):
    return lax.dot_general(a, b, (((0,), (0,)), ((), ())), preferred_element_type=jnp.float32)


def offset(i, n):
    z_size = n // X_SIZE
    a, k = i // z_size, lax.rem(i, z_size)
    dz = (k + 1) // 2 * (2 * lax.rem(k, 2) - 1)
    return lax.rem(a + k, X_SIZE), dz


def order_of(owner, me, n, sign):
    z_size = n // X_SIZE
    dx = sign * (owner // z_size - me // z_size) & (X_SIZE - 1)
    dz = sign * (owner - me) & (z_size - 1)
    k = jnp.where(dz <= z_size // 2, jnp.maximum(2 * dz - 1, 0), 2 * (z_size - dz))
    return ((dx - k) & (X_SIZE - 1)) * z_size + k


def relative_slots(label_ref, owner_rows, me, n, sign, capacity, slot_ref):
    clusters = owner_rows.shape[1]
    upper = hot(iota((128, 128), 0) <= iota((128, 128), 1))
    seen = jnp.zeros((n, 1), jnp.float32)
    for start in range(0, label_ref.shape[1], 128):
        labels = label_ref[0:1, start : start + 128]
        cluster_hot = hot(iota((clusters, 128), 0) == labels)
        owner = jnp.dot(owner_rows, cluster_hot, preferred_element_type=jnp.float32)[0:1]
        relative = order_of(owner.astype(jnp.int32), me, n, sign)
        match = iota((n, 128), 0) == relative
        owner_hot = jnp.where(match, 1.0, 0.0)
        counts = jnp.dot(
            owner_hot.astype(jnp.bfloat16), upper, preferred_element_type=jnp.float32
        )
        rank = jnp.sum(jnp.where(match, counts + seen, 0.0), axis=0, keepdims=True) - 1.0
        slot_ref[0:1, start : start + 128] = relative * capacity + rank.astype(jnp.int32)
        seen = seen + jnp.sum(owner_hot, axis=1, keepdims=True)


def exchange_kernel(
    n, n_head, q_ref, k_ref, v_ref, w_ref, qc_ref, kc_ref, owner_ref, bias_ref, out_ref,
    sq, rq, slab, rlab, sk, rk, sv, rv, so, ro, q_slot, k_slot, key_hot, probs,
    pieces, weight, mixed_in,
    send_sem, recv_sem, piece_send, piece_recv, w_send, w_recv, a_send, a_recv,
):
    me = lax.axis_index("seq")
    head = lax.axis_index("head")
    parts = n // n_head
    depth = w_ref.shape[0] // parts
    z_size = n // X_SIZE
    x, z = me // z_size, lax.rem(me, z_size)
    q_rows, k_rows = q_ref.shape[0], k_ref.shape[0]
    q_cap, k_cap = 2 * q_rows // n, 2 * k_rows // n
    heads, clusters = bias_ref.shape[0], bias_ref.shape[1]
    per_chunk = CHUNK // k_cap
    slots_q, slots_k = n * q_cap, n * k_cap

    def at(dx, dz):
        return lax.rem(x + dx + X_SIZE, X_SIZE) * z_size + lax.rem(z + dz + z_size, z_size)

    mirror = 1 - 2 * lax.rem(head, 2)

    def peer(i, back=1):
        dx, dz = offset(i, n)
        return at(back * mirror * dx, back * mirror * dz)

    def copy(kind, i):
        returning = kind >= O
        source, target, rows = {
            Q: (sq, rq, q_cap), K: (sk, rk, k_cap), V: (sv, rv, k_cap), LAB: (slab, rlab, 0),
        }.get(kind, (so, ro, q_cap))
        first = (kind - O) * slots_q if returning else 0
        window = pl.ds(pl.multiple_of(first + i * rows, rows), rows) if rows else i
        return pltpu.make_async_remote_copy(
            src_ref=source.at[window],
            dst_ref=target.at[window],
            send_sem=send_sem.at[kind, i],
            recv_sem=recv_sem.at[kind, i],
            device_id={"seq": peer(i, -1) if returning else peer(i)},
            device_id_type=MESH,
        )

    here = me // parts == head

    def piece_copy(j):
        return pltpu.make_async_remote_copy(
            src_ref=w_ref.at[pl.ds(j * depth, depth)],
            dst_ref=pieces.at[lax.rem(me, parts)],
            send_sem=piece_send.at[j],
            recv_sem=piece_recv.at[lax.rem(me, parts)],
            device_id={"seq": parts * head + j, "head": me // parts},
            device_id_type=MESH,
        )

    def piece_stays(j):
        return here & (lax.rem(me, parts) == j)

    def piece_local(j):
        return pltpu.make_async_copy(
            w_ref.at[pl.ds(j * depth, depth)], pieces.at[j], piece_recv.at[j]
        )

    def weight_copy(block, target, index, first=0, rows=None, arrival=None):
        rows = rows or depth
        window = pl.ds(pl.multiple_of(block * depth + first, rows), rows)
        return pltpu.make_async_remote_copy(
            src_ref=weight.at[window],
            dst_ref=weight.at[window],
            send_sem=w_send.at[index],
            recv_sem=w_recv.at[block if arrival is None else arrival],
            device_id={"seq": target},
            device_id_type=MESH,
        )

    far = z_size // 2

    def z_copy(distance, way):
        block, target = at(0, way * (1 - distance)), at(0, way)
        index = 2 * (distance - 1) + (1 - way) // 2
        if distance < far:
            return weight_copy(block, target, index)
        return weight_copy(block, target, index, *far_half(way))

    def far_half(way):
        return (0, depth // 2, None) if way > 0 else (depth // 2, depth // 2, n)

    def wait_z(distance):
        for way in (1, -1):
            half = far_half(way) if distance == far else ()
            weight_copy(at(0, -way * distance), me, 0, *half).wait_recv()

    def x_first_copy(dz, i):
        return weight_copy(at(0, dz), at(1 - 2 * i, 0), z_size + 2 * (dz % z_size) + i)

    def x_second_copy(dz):
        step = 1 - 2 * (dz % 2)
        return weight_copy(at(-step, dz), at(step, 0), 3 * z_size + dz % z_size)

    def wait_block(block):
        weight_copy(block, me, 0).wait_recv()

    def ring_step(distance):
        wait_z(distance)
        blocks = (far,) if distance == far else (distance, -distance)
        if distance < far:
            for way in (1, -1):
                z_copy(distance + 1, way).start()
        for dz in blocks:
            for i in range(2):
                x_first_copy(dz, i).start()

    def x_step(dz):
        wait_block(at(1, dz))
        wait_block(at(-1, dz))
        x_second_copy(dz).start()

    mate = head + 1 - 2 * lax.rem(head, 2)

    def along(t):
        return lax.rem(head + 2 * t, n_head)

    def block_copy(part, block, target, index):
        return pltpu.make_async_remote_copy(
            src_ref=mixed_in.at[block, part],
            dst_ref=mixed_in.at[block, part],
            send_sem=a_send.at[part, index],
            recv_sem=a_recv.at[part, block],
            device_id={"head": target},
            device_id_type=MESH,
        )

    barrier = pltpu.get_barrier_semaphore()
    ys = n_head // 2
    for t in range(1, ys):
        pl.semaphore_signal(barrier, inc=1, device_id={"head": along(t)}, device_id_type=MESH)
    pl.semaphore_signal(barrier, inc=1, device_id={"head": mate}, device_id_type=MESH)
    for j in range(parts):

        @pl.when(jnp.logical_not(piece_stays(j)))
        def _():
            pl.semaphore_signal(
                barrier, inc=1, device_id={"seq": parts * head + j, "head": me // parts},
                device_id_type=MESH,
            )

    @pl.loop(1, n)
    def _(i):
        pl.semaphore_signal(barrier, inc=1, device_id={"seq": peer(i)}, device_id_type=MESH)

    owner_rows = jnp.broadcast_to(
        owner_ref[...].astype(jnp.float32), (8, clusters)
    ).astype(jnp.bfloat16)
    relative_slots(qc_ref, owner_rows, me, n, mirror, q_cap, q_slot)
    relative_slots(kc_ref, owner_rows, me, n, mirror, k_cap, k_slot)

    pack_q = hot(iota((slots_q, q_rows), 0) == q_slot[...])
    sq[...] = jnp.dot(pack_q, q_ref[...], preferred_element_type=jnp.float32).astype(sq.dtype)
    q_labels = jnp.broadcast_to(
        (qc_ref[...] + 1).astype(jnp.float32), (8, q_rows)
    ).astype(jnp.bfloat16)
    packed = dot_nt(q_labels, pack_q)
    per_row = 128 // q_cap
    for i in range(n):
        group = i // per_row * 128
        slab[i, 1:2, :] = packed[0:1, group : group + 128]
    k_labels = jnp.broadcast_to(
        (kc_ref[...] + 1).astype(jnp.float32), (8, k_rows)
    ).astype(jnp.bfloat16)

    @pl.when(here)
    def _():
        pl.semaphore_wait(barrier, n - 1 + ys + parts - 1)

    @pl.when(jnp.logical_not(here))
    def _():
        pl.semaphore_wait(barrier, n - 1 + ys + parts)

    for j in range(parts):

        @pl.when(piece_stays(j))
        def _():
            piece_local(j).start()

        @pl.when(jnp.logical_not(piece_stays(j)))
        def _():
            piece_copy(j).start()

    @pl.loop(0, slots_k // CHUNK)
    def _(j):
        base = pl.multiple_of(j * CHUNK, CHUNK)
        pack = hot(iota((CHUNK, k_rows), 0) + base == k_slot[...])
        sk[pl.ds(base, CHUNK), :] = jnp.dot(
            pack, k_ref[...], preferred_element_type=jnp.float32
        ).astype(sk.dtype)
        labels = dot_nt(k_labels, pack)
        for t in range(per_chunk):
            first = t * k_cap // 128 * 128
            slab[j * per_chunk + t, 0:1, :] = labels[0:1, first : first + 128]
        for t in range(per_chunk):
            i = j * per_chunk + t

            @pl.when(i > 0)
            def _():
                copy(LAB, i).start()
                copy(Q, i).start()
                copy(K, i).start()

    for j in range(parts):
        piece_local(j).wait()
    weight[pl.ds(pl.multiple_of(me * depth, depth), depth), :] = jnp.concatenate(
        [pieces[j] for j in range(parts)], axis=1
    )
    for way in (1, -1):
        z_copy(1, way).start()
    for i in range(2):
        x_first_copy(0, i).start()

    chunks = slots_k // CHUNK

    @pl.loop(0, chunks)
    def _(j):
        base = pl.multiple_of(j * CHUNK, CHUNK)
        pack = hot(iota((CHUNK, k_rows), 0) + base == k_slot[...])
        sv[pl.ds(base, CHUNK), :] = jnp.dot(
            pack, v_ref[...], preferred_element_type=jnp.float32
        ).astype(sv.dtype)
        for t in range(per_chunk):
            i = j * per_chunk + t

            @pl.when(i > 0)
            def _():
                copy(V, i).start()

        for distance in range(1, far):

            @pl.when(j == chunks * distance // far)
            def _():
                ring_step(distance)

    ring_step(far)

    rq[0:q_cap, :] = sq[0:q_cap, :]
    rk[0:k_cap, :] = sk[0:k_cap, :]
    rv[0:k_cap, :] = sv[0:k_cap, :]
    rlab[0] = slab[0]

    @pl.loop(1, n)
    def _(i):
        copy(LAB, i).wait_recv()
        copy(Q, i).wait_recv()
        copy(K, i).wait_recv()

    lane = iota((1, 128), 1)
    q_row = []
    for first in range(0, n, per_row):
        row = jnp.zeros((1, 128), jnp.float32)
        for i in range(first, first + per_row):
            row = jnp.where(lane // q_cap == i % per_row, rlab[i, 1:2, :], row)
        q_row.append(row)
    query_hot = [
        hot(iota((clusters, 128), 0) == row.astype(jnp.int32) - 1) for row in q_row
    ]
    query_hot = jnp.concatenate(query_hot, axis=1)
    per_lanes = 128 // k_cap
    for first in range(0, n, per_lanes):
        row = rlab[first, 0:1, :]
        for i in range(first + 1, first + per_lanes):
            row = jnp.where(lane // k_cap == i % per_lanes, rlab[i, 0:1, :], row)
        row = row.astype(jnp.int32) - 1
        key_hot[:, first * k_cap : first * k_cap + 128] = hot(
            (iota((clusters, 128), 0) == row) | (row < 0)
        )

    exponent = 1.0 / math.sqrt(HEAD_SIZE) / math.log(2.0)
    half = slots_q // 2

    def columns(h):
        return pl.ds(pl.multiple_of(h * HEAD_SIZE, HEAD_SIZE), HEAD_SIZE)

    @pl.loop(0, heads)
    def _(h):
        selected = dot_tn(query_hot, bias_ref[h]).astype(jnp.bfloat16)
        for part in range(2):
            rows = slice(part * half, (part + 1) * half)
            scores = dot_nt(rq[rows, columns(h)], rk[:, columns(h)])
            scores = scores + jnp.dot(
                selected[rows], key_hot[...], preferred_element_type=jnp.float32
            )
            largest = jnp.maximum(jnp.max(scores, axis=1, keepdims=True), 0.0)
            weights = jnp.exp2((scores - largest) * exponent)
            total = jnp.exp2(-largest * exponent) + jnp.sum(weights, axis=1, keepdims=True)
            probs[h, rows, :] = (weights * (1.0 / total)).astype(jnp.bfloat16)

    for dz in (0, 1, -1, 2, -2):
        x_step(dz)

    @pl.loop(1, n)
    def _(i):
        copy(V, i).wait_recv()

    for part in range(2):

        @pl.loop(0, heads // 2)
        def _(h):
            g = h + part * (heads // 2)
            so[part * slots_q : (part + 1) * slots_q, columns(h)] = jnp.dot(
                probs[g], rv[:, columns(g)], preferred_element_type=jnp.float32
            ).astype(so.dtype)

        @pl.loop(1, n)
        def _(i):
            copy(O + part, i).start()

        own = slice(part * slots_q, part * slots_q + q_cap)
        ro[own, :] = so[own, :]

    for dz in (3, -3, far):
        x_step(dz)

    unpack = hot(iota((slots_q, q_rows), 0) == q_slot[...])
    for part in range(2):

        @pl.loop(1, n)
        def _(i):
            copy(O + part, i).wait_recv()

        mixed_in[head, part] = dot_tn(
            unpack, ro[part * slots_q : (part + 1) * slots_q, :]
        ).astype(mixed_in.dtype)
        for t in range(1, ys):
            block_copy(part, head, along(t), t - 1).start()
        block_copy(part, head, mate, ys - 1).start()

    for dz in range(z_size):
        wait_block(at(2, dz))

    def product(part, block):
        width = mixed_in.shape[3]
        rows = pl.ds(pl.multiple_of((2 * block + part) * width, width), width)
        return jnp.dot(
            mixed_in[block, part], weight[rows, :], preferred_element_type=jnp.float32
        )

    total = product(0, head) + product(1, head)
    for part in range(2):
        for t in range(1, ys):
            block_copy(part, along(t), mate, 0).wait_recv()
            block_copy(part, along(t), mate, ys - 1 + t).start()
            total = total + product(part, along(t))
    for part in range(2):
        for t in range(ys):
            block = lax.rem(mate + 2 * t, n_head)
            block_copy(part, block, mate, 0).wait_recv()
            total = total + product(part, block)
    out_ref[...] = total.astype(out_ref.dtype)

    @pl.loop(1, n)
    def _(i):
        for kind in (LAB, Q, K, V, O, O + 1):
            copy(kind, i).wait_send()

    for j in range(parts):

        @pl.when(jnp.logical_not(piece_stays(j)))
        def _():
            piece_copy(j).wait_send()

    for way in (1, -1):
        for distance in range(1, far + 1):
            z_copy(distance, way).wait_send()
    for dz in range(z_size):
        for i in range(2):
            x_first_copy(dz, i).wait_send()
        x_second_copy(dz).wait_send()
    for part in range(2):
        for t in range(1, ys):
            block_copy(part, head, along(t), t - 1).wait_send()
            block_copy(part, along(t), mate, ys - 1 + t).wait_send()
        block_copy(part, head, mate, ys - 1).wait_send()


def mix(queries, keys, values, out_weight, query_cluster, key_cluster, cluster_owner, bias):
    n, n_head = lax.axis_size("seq"), lax.axis_size("head")
    parts = n // n_head
    depth, narrow = out_weight.shape[0] // parts, out_weight.shape[1]
    q_rows, width = queries.shape
    k_rows = keys.shape[0]
    slots_q, slots_k = 2 * q_rows, 2 * k_rows
    heads, clusters = bias.shape[0], bias.shape[1]
    vmem = pl.BlockSpec(memory_space=pltpu.VMEM)

    def rows(count):
        return pltpu.VMEM((count, width), jnp.bfloat16)

    return pl.pallas_call(
        functools.partial(exchange_kernel, n, n_head),
        out_shape=jax.ShapeDtypeStruct((q_rows, narrow * parts), jnp.bfloat16),
        in_specs=[vmem] * 8,
        out_specs=vmem,
        scratch_shapes=[
            rows(slots_q), rows(slots_q),
            pltpu.VMEM((n, 8, 128), jnp.float32), pltpu.VMEM((n, 8, 128), jnp.float32),
            rows(slots_k), rows(slots_k), rows(slots_k), rows(slots_k),
            pltpu.VMEM((2 * slots_q, width // 2), jnp.bfloat16),
            pltpu.VMEM((2 * slots_q, width // 2), jnp.bfloat16),
            pltpu.VMEM((1, q_rows), jnp.int32), pltpu.VMEM((1, k_rows), jnp.int32),
            pltpu.VMEM((clusters, slots_k), jnp.bfloat16),
            pltpu.VMEM((heads, slots_q, slots_k), jnp.bfloat16),
            pltpu.VMEM((parts, depth, narrow), jnp.bfloat16),
            pltpu.VMEM((depth * n, narrow * parts), jnp.bfloat16),
            pltpu.VMEM((n_head, 2, q_rows, width // 2), jnp.bfloat16),
            pltpu.SemaphoreType.DMA((6, n)), pltpu.SemaphoreType.DMA((6, n)),
            pltpu.SemaphoreType.DMA((parts,)), pltpu.SemaphoreType.DMA((parts,)),
            pltpu.SemaphoreType.DMA((n,)), pltpu.SemaphoreType.DMA((n + 1,)),
            pltpu.SemaphoreType.DMA((2, n_head)), pltpu.SemaphoreType.DMA((2, n_head)),
        ],
        compiler_params=pltpu.CompilerParams(
            collective_id=0, has_side_effects=True, vmem_limit_bytes=60 * 2**20
        ),
        cost_estimate=pl.CostEstimate(
            flops=2 * 10**11, bytes_accessed=16 * 2**20, transcendentals=0
        ),
    )(
        queries, keys, values, out_weight, query_cluster[None], key_cluster[None],
        cluster_owner[None], bias,
    )


def per_device(
    queries, keys, values, query_cluster, key_cluster, cluster_owner, pair_list, out_weight
):
    clusters = cluster_owner.shape[0]
    listed = jnp.any(
        pair_list[:, :, :, None] == jnp.arange(clusters, dtype=jnp.int32)[None, None, None, :],
        axis=2,
    )
    bias = jnp.where(listed, 0.0, MASKED).astype(jnp.bfloat16)
    return mix(
        queries, keys, values, out_weight, query_cluster, key_cluster, cluster_owner, bias
    )


def solution(mesh):
    in_specs = (
        P("seq", "head"),
        P("seq", "head"),
        P("seq", "head"),
        P("seq"),
        P("seq"),
        P(),
        P("head", None, None),
        P("head", "seq"),
    )
    out_specs = P("seq", "head")
    return jax.shard_map(
        per_device, mesh=mesh, in_specs=in_specs, out_specs=out_specs, check_vma=False
    )
```

```python
import functools
import math

import jax
import jax.numpy as jnp
from jax import lax
from jax.experimental import pallas as pl
from jax.experimental.pallas import tpu as pltpu
from jax.sharding import PartitionSpec as P

MESH = pl.DeviceIdType.MESH
HEAD_SIZE = 128
MASKED = -float(2**20)
CHUNK = 256

Q, LAB, K, V, O = range(5)
X_SIZE = 4


def iota(shape, dim):
    return lax.broadcasted_iota(jnp.int32, shape, dim)


def hot(mask):
    return jnp.where(mask, 1.0, 0.0).astype(jnp.bfloat16)


def dot_nt(a, b):
    return lax.dot_general(a, b, (((1,), (1,)), ((), ())), preferred_element_type=jnp.float32)


def dot_tn(a, b):
    return lax.dot_general(a, b, (((0,), (0,)), ((), ())), preferred_element_type=jnp.float32)


def offset(i, n):
    z_size = n // X_SIZE
    a, k = i // z_size, lax.rem(i, z_size)
    dz = (k + 1) // 2 * (2 * lax.rem(k, 2) - 1)
    return lax.rem(a + k, X_SIZE), dz


def order_of(owner, me, n, sign):
    z_size = n // X_SIZE
    dx = sign * (owner // z_size - me // z_size) & (X_SIZE - 1)
    dz = sign * (owner - me) & (z_size - 1)
    k = jnp.where(dz <= z_size // 2, jnp.maximum(2 * dz - 1, 0), 2 * (z_size - dz))
    return ((dx - k) & (X_SIZE - 1)) * z_size + k


def relative_slots(label_ref, owner_rows, me, n, sign, capacity, slot_ref):
    clusters = owner_rows.shape[1]
    upper = hot(iota((128, 128), 0) <= iota((128, 128), 1))
    seen = jnp.zeros((n, 1), jnp.float32)
    for start in range(0, label_ref.shape[1], 128):
        labels = label_ref[0:1, start : start + 128]
        cluster_hot = hot(iota((clusters, 128), 0) == labels)
        owner = jnp.dot(owner_rows, cluster_hot, preferred_element_type=jnp.float32)[0:1]
        relative = order_of(owner.astype(jnp.int32), me, n, sign)
        match = iota((n, 128), 0) == relative
        owner_hot = jnp.where(match, 1.0, 0.0)
        counts = jnp.dot(
            owner_hot.astype(jnp.bfloat16), upper, preferred_element_type=jnp.float32
        )
        rank = jnp.sum(jnp.where(match, counts + seen, 0.0), axis=0, keepdims=True) - 1.0
        slot_ref[0:1, start : start + 128] = relative * capacity + rank.astype(jnp.int32)
        seen = seen + jnp.sum(owner_hot, axis=1, keepdims=True)


def exchange_kernel(
    n, n_head, q_ref, k_ref, v_ref, w_ref, qc_ref, kc_ref, owner_ref, bias_ref, out_ref,
    sq, rq, slab, rlab, sk, rk, sv, rv, so, ro, q_slot, k_slot, key_hot, probs,
    pieces, weight, mixed_in,
    send_sem, recv_sem, piece_send, piece_recv, w_send, w_recv, a_send, a_recv,
):
    me = lax.axis_index("seq")
    head = lax.axis_index("head")
    parts = n // n_head
    depth = w_ref.shape[0] // parts
    z_size = n // X_SIZE
    x, z = me // z_size, lax.rem(me, z_size)
    q_rows, k_rows = q_ref.shape[0], k_ref.shape[0]
    q_cap, k_cap = 2 * q_rows // n, 2 * k_rows // n
    heads, clusters = bias_ref.shape[0], bias_ref.shape[1]
    per_chunk = CHUNK // k_cap
    slots_q, slots_k = n * q_cap, n * k_cap

    def at(dx, dz):
        return lax.rem(x + dx + X_SIZE, X_SIZE) * z_size + lax.rem(z + dz + z_size, z_size)

    mirror = 1 - 2 * lax.rem(head, 2)

    def peer(i, back=1):
        dx, dz = offset(i, n)
        return at(back * mirror * dx, back * mirror * dz)

    def copy(kind, i):
        returning = kind >= O
        source, target, rows = {
            Q: (sq, rq, q_cap), K: (sk, rk, k_cap), V: (sv, rv, k_cap), LAB: (slab, rlab, 0),
        }.get(kind, (so, ro, q_cap))
        first = (kind - O) * slots_q if returning else 0
        window = pl.ds(pl.multiple_of(first + i * rows, rows), rows) if rows else i
        return pltpu.make_async_remote_copy(
            src_ref=source.at[window],
            dst_ref=target.at[window],
            send_sem=send_sem.at[kind, i],
            recv_sem=recv_sem.at[kind, i],
            device_id={"seq": peer(i, -1) if returning else peer(i)},
            device_id_type=MESH,
        )

    here = me // parts == head

    def piece_copy(j):
        return pltpu.make_async_remote_copy(
            src_ref=w_ref.at[pl.ds(j * depth, depth)],
            dst_ref=pieces.at[lax.rem(me, parts)],
            send_sem=piece_send.at[j],
            recv_sem=piece_recv.at[lax.rem(me, parts)],
            device_id={"seq": parts * head + j, "head": me // parts},
            device_id_type=MESH,
        )

    def piece_stays(j):
        return here & (lax.rem(me, parts) == j)

    def piece_local(j):
        return pltpu.make_async_copy(
            w_ref.at[pl.ds(j * depth, depth)], pieces.at[j], piece_recv.at[j]
        )

    def weight_copy(block, target, index, first=0, rows=None, arrival=None):
        rows = rows or depth
        window = pl.ds(pl.multiple_of(block * depth + first, rows), rows)
        return pltpu.make_async_remote_copy(
            src_ref=weight.at[window],
            dst_ref=weight.at[window],
            send_sem=w_send.at[index],
            recv_sem=w_recv.at[block if arrival is None else arrival],
            device_id={"seq": target},
            device_id_type=MESH,
        )

    far = z_size // 2

    def z_copy(distance, way):
        block, target = at(0, way * (1 - distance)), at(0, way)
        index = 2 * (distance - 1) + (1 - way) // 2
        if distance < far:
            return weight_copy(block, target, index)
        return weight_copy(block, target, index, *far_half(way))

    def far_half(way):
        return (0, depth // 2, None) if way > 0 else (depth // 2, depth // 2, n)

    def wait_z(distance):
        for way in (1, -1):
            half = far_half(way) if distance == far else ()
            weight_copy(at(0, -way * distance), me, 0, *half).wait_recv()

    def x_first_copy(dz, i):
        return weight_copy(at(0, dz), at(1 - 2 * i, 0), z_size + 2 * (dz % z_size) + i)

    def x_second_copy(dz):
        step = 1 - 2 * (dz % 2)
        return weight_copy(at(-step, dz), at(step, 0), 3 * z_size + dz % z_size)

    def wait_block(block):
        weight_copy(block, me, 0).wait_recv()

    def ring_step(distance):
        wait_z(distance)
        blocks = (far,) if distance == far else (distance, -distance)
        if distance < far:
            for way in (1, -1):
                z_copy(distance + 1, way).start()
        for dz in blocks:
            for i in range(2):
                x_first_copy(dz, i).start()

    z_order = (0, 1, -1, 2, -2, 3, -3, far)

    def x_step(dz):
        wait_block(at(1, dz))
        wait_block(at(-1, dz))
        x_second_copy(dz).start()

    mate = head + 1 - 2 * lax.rem(head, 2)

    def along(t):
        return lax.rem(head + 2 * t, n_head)

    def block_copy(part, block, target, index):
        return pltpu.make_async_remote_copy(
            src_ref=mixed_in.at[block, part],
            dst_ref=mixed_in.at[block, part],
            send_sem=a_send.at[part, index],
            recv_sem=a_recv.at[part, block],
            device_id={"head": target},
            device_id_type=MESH,
        )

    barrier = pltpu.get_barrier_semaphore()
    ys = n_head // 2
    for t in range(1, ys):
        pl.semaphore_signal(barrier, inc=1, device_id={"head": along(t)}, device_id_type=MESH)
    pl.semaphore_signal(barrier, inc=1, device_id={"head": mate}, device_id_type=MESH)
    for j in range(parts):

        @pl.when(jnp.logical_not(piece_stays(j)))
        def _():
            pl.semaphore_signal(
                barrier, inc=1, device_id={"seq": parts * head + j, "head": me // parts},
                device_id_type=MESH,
            )

    @pl.loop(1, n)
    def _(i):
        pl.semaphore_signal(barrier, inc=1, device_id={"seq": peer(i)}, device_id_type=MESH)

    owner_rows = jnp.broadcast_to(
        owner_ref[...].astype(jnp.float32), (8, clusters)
    ).astype(jnp.bfloat16)
    relative_slots(qc_ref, owner_rows, me, n, mirror, q_cap, q_slot)
    relative_slots(kc_ref, owner_rows, me, n, mirror, k_cap, k_slot)

    pack_q = hot(iota((slots_q, q_rows), 0) == q_slot[...])
    sq[...] = jnp.dot(pack_q, q_ref[...], preferred_element_type=jnp.float32).astype(sq.dtype)
    q_labels = jnp.broadcast_to(
        (qc_ref[...] + 1).astype(jnp.float32), (8, q_rows)
    ).astype(jnp.bfloat16)
    packed = dot_nt(q_labels, pack_q)
    per_row = 128 // q_cap
    for i in range(n):
        group = i // per_row * 128
        slab[i, 1:2, :] = packed[0:1, group : group + 128]
    k_labels = jnp.broadcast_to(
        (kc_ref[...] + 1).astype(jnp.float32), (8, k_rows)
    ).astype(jnp.bfloat16)

    @pl.when(here)
    def _():
        pl.semaphore_wait(barrier, n - 1 + ys + parts - 1)

    @pl.when(jnp.logical_not(here))
    def _():
        pl.semaphore_wait(barrier, n - 1 + ys + parts)

    for j in range(parts):

        @pl.when(piece_stays(j))
        def _():
            piece_local(j).start()

        @pl.when(jnp.logical_not(piece_stays(j)))
        def _():
            piece_copy(j).start()

    @pl.loop(0, slots_k // CHUNK)
    def _(j):
        base = pl.multiple_of(j * CHUNK, CHUNK)
        pack = hot(iota((CHUNK, k_rows), 0) + base == k_slot[...])
        sk[pl.ds(base, CHUNK), :] = jnp.dot(
            pack, k_ref[...], preferred_element_type=jnp.float32
        ).astype(sk.dtype)
        labels = dot_nt(k_labels, pack)
        for t in range(per_chunk):
            first = t * k_cap // 128 * 128
            slab[j * per_chunk + t, 0:1, :] = labels[0:1, first : first + 128]
        for t in range(per_chunk):
            i = j * per_chunk + t

            @pl.when(i > 0)
            def _():
                copy(LAB, i).start()
                copy(Q, i).start()
                copy(K, i).start()

    for j in range(parts):
        piece_local(j).wait()
    weight[pl.ds(pl.multiple_of(me * depth, depth), depth), :] = jnp.concatenate(
        [pieces[j] for j in range(parts)], axis=1
    )
    for way in (1, -1):
        z_copy(1, way).start()
    for i in range(2):
        x_first_copy(0, i).start()

    chunks = slots_k // CHUNK

    @pl.loop(0, chunks)
    def _(j):
        base = pl.multiple_of(j * CHUNK, CHUNK)
        pack = hot(iota((CHUNK, k_rows), 0) + base == k_slot[...])
        sv[pl.ds(base, CHUNK), :] = jnp.dot(
            pack, v_ref[...], preferred_element_type=jnp.float32
        ).astype(sv.dtype)
        for t in range(per_chunk):
            i = j * per_chunk + t

            @pl.when(i > 0)
            def _():
                copy(V, i).start()

        for distance in range(1, far):

            @pl.when(j == chunks * distance // far)
            def _():
                ring_step(distance)

    ring_step(far)

    rq[0:q_cap, :] = sq[0:q_cap, :]
    rk[0:k_cap, :] = sk[0:k_cap, :]
    rv[0:k_cap, :] = sv[0:k_cap, :]
    rlab[0] = slab[0]

    @pl.loop(1, n)
    def _(i):
        copy(LAB, i).wait_recv()
        copy(Q, i).wait_recv()
        copy(K, i).wait_recv()

    lane = iota((1, 128), 1)
    q_row = []
    for first in range(0, n, per_row):
        row = jnp.zeros((1, 128), jnp.float32)
        for i in range(first, first + per_row):
            row = jnp.where(lane // q_cap == i % per_row, rlab[i, 1:2, :], row)
        q_row.append(row)
    query_hot = [
        hot(iota((clusters, 128), 0) == row.astype(jnp.int32) - 1) for row in q_row
    ]
    query_hot = jnp.concatenate(query_hot, axis=1)
    per_lanes = 128 // k_cap
    for first in range(0, n, per_lanes):
        row = rlab[first, 0:1, :]
        for i in range(first + 1, first + per_lanes):
            row = jnp.where(lane // k_cap == i % per_lanes, rlab[i, 0:1, :], row)
        row = row.astype(jnp.int32) - 1
        key_hot[:, first * k_cap : first * k_cap + 128] = hot(
            (iota((clusters, 128), 0) == row) | (row < 0)
        )

    exponent = 1.0 / math.sqrt(HEAD_SIZE) / math.log(2.0)
    half = slots_q // 2

    def columns(h):
        return pl.ds(pl.multiple_of(h * HEAD_SIZE, HEAD_SIZE), HEAD_SIZE)

    @pl.loop(0, heads)
    def _(h):
        selected = dot_tn(query_hot, bias_ref[h]).astype(jnp.bfloat16)
        for part in range(2):
            rows = slice(part * half, (part + 1) * half)
            scores = dot_nt(rq[rows, columns(h)], rk[:, columns(h)])
            scores = scores + jnp.dot(
                selected[rows], key_hot[...], preferred_element_type=jnp.float32
            )
            largest = jnp.maximum(jnp.max(scores, axis=1, keepdims=True), 0.0)
            weights = jnp.exp2((scores - largest) * exponent)
            total = jnp.exp2(-largest * exponent) + jnp.sum(weights, axis=1, keepdims=True)
            probs[h, rows, :] = (weights * (1.0 / total)).astype(jnp.bfloat16)

    @pl.loop(1, n)
    def _(i):
        copy(V, i).wait_recv()

    for part in range(2):

        @pl.loop(0, heads // 2)
        def _(h):
            g = h + part * (heads // 2)
            so[part * slots_q : (part + 1) * slots_q, columns(h)] = jnp.dot(
                probs[g], rv[:, columns(g)], preferred_element_type=jnp.float32
            ).astype(so.dtype)

        @pl.loop(1, n)
        def _(i):
            copy(O + part, i).start()

        own = slice(part * slots_q, part * slots_q + q_cap)
        ro[own, :] = so[own, :]

    for dz in z_order:
        x_step(dz)

    unpack = hot(iota((slots_q, q_rows), 0) == q_slot[...])
    for part in range(2):

        @pl.loop(1, n)
        def _(i):
            copy(O + part, i).wait_recv()

        mixed_in[head, part] = dot_tn(
            unpack, ro[part * slots_q : (part + 1) * slots_q, :]
        ).astype(mixed_in.dtype)
        for t in range(1, ys):
            block_copy(part, head, along(t), t - 1).start()
        block_copy(part, head, mate, ys - 1).start()

    for dz in range(z_size):
        wait_block(at(2, dz))

    def product(part, block):
        width = mixed_in.shape[3]
        rows = pl.ds(pl.multiple_of((2 * block + part) * width, width), width)
        return jnp.dot(
            mixed_in[block, part], weight[rows, :], preferred_element_type=jnp.float32
        )

    total = product(0, head) + product(1, head)
    for part in range(2):
        for t in range(1, ys):
            block_copy(part, along(t), mate, 0).wait_recv()
            block_copy(part, along(t), mate, ys - 1 + t).start()
            total = total + product(part, along(t))
    for part in range(2):
        for t in range(ys):
            block = lax.rem(mate + 2 * t, n_head)
            block_copy(part, block, mate, 0).wait_recv()
            total = total + product(part, block)
    out_ref[...] = total.astype(out_ref.dtype)

    @pl.loop(1, n)
    def _(i):
        for kind in (LAB, Q, K, V, O, O + 1):
            copy(kind, i).wait_send()

    for j in range(parts):

        @pl.when(jnp.logical_not(piece_stays(j)))
        def _():
            piece_copy(j).wait_send()

    for way in (1, -1):
        for distance in range(1, far + 1):
            z_copy(distance, way).wait_send()
    for dz in range(z_size):
        for i in range(2):
            x_first_copy(dz, i).wait_send()
        x_second_copy(dz).wait_send()
    for part in range(2):
        for t in range(1, ys):
            block_copy(part, head, along(t), t - 1).wait_send()
            block_copy(part, along(t), mate, ys - 1 + t).wait_send()
        block_copy(part, head, mate, ys - 1).wait_send()


def mix(queries, keys, values, out_weight, query_cluster, key_cluster, cluster_owner, bias):
    n, n_head = lax.axis_size("seq"), lax.axis_size("head")
    parts = n // n_head
    depth, narrow = out_weight.shape[0] // parts, out_weight.shape[1]
    q_rows, width = queries.shape
    k_rows = keys.shape[0]
    slots_q, slots_k = 2 * q_rows, 2 * k_rows
    heads, clusters = bias.shape[0], bias.shape[1]
    vmem = pl.BlockSpec(memory_space=pltpu.VMEM)

    def rows(count):
        return pltpu.VMEM((count, width), jnp.bfloat16)

    return pl.pallas_call(
        functools.partial(exchange_kernel, n, n_head),
        out_shape=jax.ShapeDtypeStruct((q_rows, narrow * parts), jnp.bfloat16),
        in_specs=[vmem] * 8,
        out_specs=vmem,
        scratch_shapes=[
            rows(slots_q), rows(slots_q),
            pltpu.VMEM((n, 8, 128), jnp.float32), pltpu.VMEM((n, 8, 128), jnp.float32),
            rows(slots_k), rows(slots_k), rows(slots_k), rows(slots_k),
            pltpu.VMEM((2 * slots_q, width // 2), jnp.bfloat16),
            pltpu.VMEM((2 * slots_q, width // 2), jnp.bfloat16),
            pltpu.VMEM((1, q_rows), jnp.int32), pltpu.VMEM((1, k_rows), jnp.int32),
            pltpu.VMEM((clusters, slots_k), jnp.bfloat16),
            pltpu.VMEM((heads, slots_q, slots_k), jnp.bfloat16),
            pltpu.VMEM((parts, depth, narrow), jnp.bfloat16),
            pltpu.VMEM((depth * n, narrow * parts), jnp.bfloat16),
            pltpu.VMEM((n_head, 2, q_rows, width // 2), jnp.bfloat16),
            pltpu.SemaphoreType.DMA((6, n)), pltpu.SemaphoreType.DMA((6, n)),
            pltpu.SemaphoreType.DMA((parts,)), pltpu.SemaphoreType.DMA((parts,)),
            pltpu.SemaphoreType.DMA((n,)), pltpu.SemaphoreType.DMA((n + 1,)),
            pltpu.SemaphoreType.DMA((2, n_head)), pltpu.SemaphoreType.DMA((2, n_head)),
        ],
        compiler_params=pltpu.CompilerParams(
            collective_id=0, has_side_effects=True, vmem_limit_bytes=60 * 2**20
        ),
        cost_estimate=pl.CostEstimate(
            flops=2 * 10**11, bytes_accessed=16 * 2**20, transcendentals=0
        ),
    )(
        queries, keys, values, out_weight, query_cluster[None], key_cluster[None],
        cluster_owner[None], bias,
    )


def per_device(
    queries, keys, values, query_cluster, key_cluster, cluster_owner, pair_list, out_weight
):
    clusters = cluster_owner.shape[0]
    listed = jnp.any(
        pair_list[:, :, :, None] == jnp.arange(clusters, dtype=jnp.int32)[None, None, None, :],
        axis=2,
    )
    bias = jnp.where(listed, 0.0, MASKED).astype(jnp.bfloat16)
    return mix(
        queries, keys, values, out_weight, query_cluster, key_cluster, cluster_owner, bias
    )


def solution(mesh):
    in_specs = (
        P("seq", "head"),
        P("seq", "head"),
        P("seq", "head"),
        P("seq"),
        P("seq"),
        P(),
        P("head", None, None),
        P("head", "seq"),
    )
    out_specs = P("seq", "head")
    return jax.shard_map(
        per_device, mesh=mesh, in_specs=in_specs, out_specs=out_specs, check_vma=False
    )
```
